32 devices in a mesh: grp: 4 (over y, x), orient: 8 (over z, core).
Axes of the slice: x: 2, y: 2, z: 4, core: 2. Of those that a mesh axis runs over, the one named last changes fastest.
Arguments:
- images: bfloat16 [1024, 2, 8192], P(('grp', 'orient')), may hold values from -6 to 6
- ctf: bfloat16 [1024, 8192], P(('grp', 'orient')), may hold values from -1 to 1
- shifts: int32 [1024, 2], P(('grp', 'orient')), may hold values from -8 to 8
- home: int32 [4, 1024, 1], P(None, ('grp', 'orient')), may hold values from 0 to 7; in each aligned block of 32 rows (0 to 31, 32 to 63, ..., all dimensions but the last counted through in order) at most 8 rows name the same one
- neighbours: int32 [1024, 4, 128], P(('grp', 'orient')), may hold values from 0 to 511
- references: bfloat16 [4, 4096, 2, 8192], P('grp', 'orient'), may hold values from -6 to 6
- noise_weight: float32 [4, 8192], P('grp'), may hold values from 0.25 to 4
Outputs:
- centred: float32 [1024, 4, 128], P(('grp', 'orient'))
The draws below stay inside these ranges and needn't reach their ends.
Inputs may be any that keep to these rules, and one draw needn't show every extreme that they name: `home`: within one group, at most 8 of the 32 particles of one device share a block, and in every draw some device has exactly 8 particles in one block.
All inputs are finite; a program needn't handle non-finite values.
Results may differ from the reference program's by a relative error of at most 0.0042.
Values may be sent and summed in bfloat16 or wider, within the bound.
A program may use at most 256 MiB of HBM per device.

```python
import math
import jax
import jax.numpy as jnp
import numpy as np
from jax import lax

BOX = 128
PIX = 8192
ORI_DEV = 512
NBR = 128
PART_DEV = 32
GROUPS = 4
OWNERS = 8
CAP = 8
ORIENTS = 4096
PARTS_SIZE = 1024


def touch_ends(array, key, smallest, high):
    longest = array.shape.index(max(array.shape))
    spots = []
    for shift in (0, 1):
        where = [jax.random.randint(jax.random.fold_in(key, axis), (), 0, length) for axis, length in enumerate(array.shape)]
        where[longest] = (where[longest] + shift) % array.shape[longest]
        spots.append(tuple(where))
    return array.at[spots[0]].set(smallest).at[spots[1]].set(high)


def steps_of(stream_key, shape, cuts, smallest, top_value):
    def one(axis_at, parts):
        heights = jax.random.uniform(jax.random.fold_in(jax.random.fold_in(stream_key, 6), axis_at), (parts,), jnp.float32, smallest / len(cuts), top_value / len(cuts))
        return jnp.repeat(jnp.exp(heights), shape[axis_at] // parts).reshape((-1,) + (1,) * (len(shape) - axis_at - 1))

    level = one(*cuts[0])
    for cut in cuts[1:]:
        level = level * one(*cut)
    return level


def assign_block(rng, own, number, rows, number_of, top, reach, skew):
    ranking = jax.random.permutation(rng, number_of)
    crowded, common = shares(number_of, rows * top, reach, skew, True), shares(number_of, rows * top, reach, skew, False)
    places = jnp.arange(number_of)

    def named(sizes, offset_by):
        used = int((sizes > 0).sum())
        fixed = max(1, used // 4)
        moved = fixed + (places - fixed + offset_by * (used - fixed)) % max(1, number_of - fixed)
        return jnp.zeros((number_of,), jnp.int32).at[ranking[jnp.where(places < fixed, places, moved)]].set(jnp.asarray(sizes, jnp.int32))

    sizes = jnp.where(number % 4 == 0, named(crowded, number // 4), named(common, number - number // 4 - 1))
    mixed = jax.random.permutation(jax.random.fold_in(own, 3), number_of)
    source_of, sink = mixed[0:number_of // 2 * 2:2], mixed[1:number_of // 2 * 2:2]
    room = jnp.minimum(sizes[source_of] - 1, reach - sizes[sink]) // 2
    room = jnp.where((source_of == ranking[0]) | (sink == ranking[0]) | (sizes[sink] == 0), 0, jnp.maximum(room, 0))
    moved = jax.random.randint(jax.random.fold_in(own, 4), (number_of // 2,), 0, 1 << 20) % (room + 1)
    sizes = sizes.at[source_of].add(-moved).at[sink].add(moved)
    members = jnp.searchsorted(jnp.cumsum(sizes), jnp.arange(rows * top), side="right").astype(jnp.int32)
    table = members.reshape(top, rows).T
    table = table[jax.random.permutation(jax.random.fold_in(own, 1), rows)]
    offset_by = jax.random.randint(jax.random.fold_in(own, 2), (rows, 1), 0, top)
    return jnp.take_along_axis(table, (jnp.arange(top)[None, :] + offset_by) % top, axis=1)


def shares(number_of, total, limit, slope, full):
    weights = [(1 << 20) // math.isqrt(rank ** slope) + 1 for rank in range(1, number_of + 1)]
    largest = limit if full else min(limit, max(-(-total // number_of), total * weights[0] // sum(weights)))
    least = 1 if total - largest >= number_of - 1 else 0
    counts, spare = [largest] + [least] * (number_of - 1), total - largest - least * (number_of - 1)
    while spare > 0:
        candidates = [i for i in range(1, number_of) if counts[i] < largest] or [i for i in range(1, number_of) if counts[i] < limit]
        pool, budget = sum([weights[i] for i in candidates]), spare
        for i in candidates:
            more = min(limit - counts[i], max(1, budget * weights[i] // pool), spare)
            counts[i] = counts[i] + more
            spare = spare - more
    return np.array(counts)


def gaussian(key, extent, width, bound, pieces=(), held_as=jnp.bfloat16):
    gain = steps_of(key, extent, pieces, -0.22, 0.18) if pieces else 1.0
    entries = jax.random.normal(key, extent, jnp.float32) * width * gain
    return jnp.minimum(jnp.maximum(entries, -bound), bound).astype(held_as)


def setup_inputs(seed: int = 0) -> dict:
    splits = jax.random.split(jax.random.key(seed), 8)
    images = gaussian(splits[0], (PARTS_SIZE, 2, PIX), 1.0, 6.0, ((0, 32),))
    ctf = jnp.clip(jax.random.uniform(splits[1], (PARTS_SIZE, PIX), jnp.float32, -1.0, 1.0) * steps_of(splits[1], (PARTS_SIZE, PIX), ((0, 32),), -0.4, 0.0), -1.0, 1.0).astype(jnp.bfloat16)
    shifts = touch_ends(jax.random.randint(splits[2], (PARTS_SIZE, 2), -8, 9), jax.random.fold_in(splits[2], 1), -8, 8).astype(jnp.int32)
    home_keys = jax.random.split(jax.random.fold_in(splits[3], 1), GROUPS * PARTS_SIZE // PART_DEV)
    home_turns = jax.random.permutation(jax.random.fold_in(splits[3], 3), GROUPS * PARTS_SIZE // PART_DEV)
    home = jax.vmap(lambda own, number: assign_block(jax.random.fold_in(splits[3], 2), own, number, PART_DEV, OWNERS, 1, CAP, 2))(home_keys, home_turns).reshape((GROUPS, PARTS_SIZE, 1))
    neighbours = touch_ends(jax.random.randint(splits[4], (PARTS_SIZE, GROUPS, NBR), 0, ORI_DEV), jax.random.fold_in(splits[4], 1), 0, ORI_DEV - 1).astype(jnp.int32)
    references = gaussian(splits[5], (GROUPS, ORIENTS, 2, PIX), 1.0, 6.0, ((0, 4), (1, 8)))
    noise_weight = jnp.clip(jnp.exp(math.log(4.0) - 2.7725887 * jax.random.uniform(splits[6], (GROUPS, PIX), jnp.float32) ** steps_of(splits[6], (GROUPS, PIX), ((0, 4),), -0.2, 0.2)), 0.25, 4.0)
    return dict(images=images, ctf=ctf, shifts=shifts, home=home, neighbours=neighbours, references=references, noise_weight=noise_weight)


def shift_tables(shifts, box):
    half = box // 2
    row = jnp.arange(box, dtype=jnp.int32)
    freq_y = jnp.where(row < half, row, row - box).astype(jnp.float32)
    freq_x = jnp.arange(half, dtype=jnp.int32).astype(jnp.float32)
    grid_y = jnp.broadcast_to(freq_y[:, None], (box, half)).reshape(-1)
    grid_x = jnp.broadcast_to(freq_x[None, :], (box, half)).reshape(-1)
    move_x = shifts[:, 0].astype(jnp.float32)
    move_y = shifts[:, 1].astype(jnp.float32)
    angle = -2.0 * math.pi / box * (move_x[:, None] * grid_x[None, :] + move_y[:, None] * grid_y[None, :])
    return (jnp.cos(angle), jnp.sin(angle))

def reference(images, ctf, shifts, home, neighbours, references, noise_weight):
    cosine, sine = shift_tables(shifts, BOX)
    real = images[:, 0].astype(jnp.float32)
    imag = images[:, 1].astype(jnp.float32)
    shifted = jnp.stack([real * cosine - imag * sine, real * sine + imag * cosine], axis=1).astype(jnp.bfloat16)
    ref_real = references[:, :, 0].astype(jnp.float32)
    ref_imag = references[:, :, 1].astype(jnp.float32)
    ref_power = (ref_real * ref_real + ref_imag * ref_imag).astype(jnp.bfloat16)
    orientation = jnp.transpose(home[:, :, 0]).astype(jnp.int32)[:, :, None] * ORI_DEV + neighbours.astype(jnp.int32)
    scale = 1.0 / math.sqrt(PIX)

    def score_one(item):
        shifted_p, ctf_p, picks_all = item
        ctf_f = ctf_p.astype(jnp.float32)

        def per_group(weight, blocks, powers, picks):
            tone = weight * ctf_f
            weighted = (tone[None, :] * shifted_p.astype(jnp.float32)).astype(jnp.bfloat16).reshape(-1)
            tone_power = (tone * ctf_f).astype(jnp.bfloat16)
            chosen = blocks[picks].reshape(picks.shape[0], -1)
            cross = jnp.dot(chosen, weighted, preferred_element_type=jnp.float32)
            power = jnp.dot(powers[picks], tone_power, preferred_element_type=jnp.float32)
            return (power - 2.0 * cross) * scale
        return jax.vmap(per_group)(noise_weight, references, ref_power, picks_all)
    score = lax.map(score_one, (shifted, ctf, orientation))
    return score - lax.optimization_barrier(jnp.mean(score, axis=2, keepdims=True))
```

```python
import functools
import math

import jax
import jax.numpy as jnp
from jax import lax
from jax.experimental import pallas as pl
from jax.experimental.pallas import tpu as pltpu
from jax.sharding import PartitionSpec as P

BOX = 128
PIX = 8192


def shift_tables(shifts, box):
    half = box // 2
    row = jnp.arange(box, dtype=jnp.int32)
    freq_y = jnp.where(row < half, row, row - box).astype(jnp.float32)
    freq_x = jnp.arange(half, dtype=jnp.int32).astype(jnp.float32)
    grid_y = jnp.broadcast_to(freq_y[:, None], (box, half)).reshape(-1)
    grid_x = jnp.broadcast_to(freq_x[None, :], (box, half)).reshape(-1)
    move_x = shifts[:, 0].astype(jnp.float32)
    move_y = shifts[:, 1].astype(jnp.float32)
    angle = (
        -2.0
        * math.pi
        / box
        * (move_x[:, None] * grid_x[None, :] + move_y[:, None] * grid_y[None, :])
    )
    return (jnp.cos(angle), jnp.sin(angle))


def pick_columns(table, lists):
    width = table.shape[-1]
    marks = (lists[..., None] == jnp.arange(width, dtype=jnp.int32)).astype(jnp.float32)
    return jnp.einsum("ano,ao->an", marks, table, precision=lax.Precision.HIGHEST)


def per_device_plain(images, ctf, shifts, home, neighbours, references, noise_weight):
    groups = home.shape[0]
    owners = lax.axis_size("orient")
    devices = groups * owners
    local = images.shape[0]
    pixels = images.shape[2]
    slots = max(2, 2 * local // owners)
    cosine, sine = shift_tables(shifts, BOX)
    real = images[:, 0].astype(jnp.float32)
    imag = images[:, 1].astype(jnp.float32)
    payload = jnp.stack(
        [real * cosine - imag * sine, real * sine + imag * cosine, ctf.astype(jnp.float32)], axis=1
    ).astype(jnp.bfloat16)
    target = home[:, :, 0]
    places = jnp.arange(owners, dtype=jnp.int32)
    hits = (target[:, :, None] == places[None, None, :]).astype(jnp.int32)
    rank = jnp.sum((jnp.cumsum(hits, axis=1) - hits) * hits, axis=2)
    slot = (jnp.arange(groups, dtype=jnp.int32)[:, None] * owners + target) * slots + rank
    total = devices * slots
    chosen = (slot[:, None, :] == jnp.arange(total, dtype=jnp.int32)[None, :, None]).astype(
        jnp.int32
    )
    select = jnp.sum(chosen, axis=0).astype(jnp.bfloat16)
    buffer = jnp.dot(select, payload.reshape(local, -1), preferred_element_type=jnp.float32).astype(
        jnp.bfloat16
    )
    buffer = buffer.reshape(devices, slots, 3, pixels)
    weight = noise_weight[0]
    blocks = references[0]
    flat_refs = blocks.reshape(blocks.shape[0], -1)
    ref_real = blocks[:, 0].astype(jnp.float32)
    ref_imag = blocks[:, 1].astype(jnp.float32)
    ref_power = (ref_real * ref_real + ref_imag * ref_imag).astype(jnp.bfloat16)
    scale = 1.0 / math.sqrt(PIX)
    contract = (((1,), (1,)), ((), ()))
    arrived = lax.all_to_all(buffer, ("grp", "orient"), split_axis=0, concat_axis=0, tiled=True)
    lead = arrived.shape[:2]
    flat = arrived.reshape(-1, 3, pixels).astype(jnp.float32)
    tone = weight[None, :] * flat[:, 2]
    weighted = (tone[:, None, :] * flat[:, :2]).astype(jnp.bfloat16).reshape(flat.shape[0], -1)
    tone_power = (tone * flat[:, 2]).astype(jnp.bfloat16)
    cross = lax.dot_general(weighted, flat_refs, contract, preferred_element_type=jnp.float32)
    power = lax.dot_general(tone_power, ref_power, contract, preferred_element_type=jnp.float32)
    table = ((power - 2.0 * cross) * scale).reshape(lead + (-1,))
    returned = lax.all_to_all(table, ("grp", "orient"), split_axis=0, concat_axis=0, tiled=True)
    flat_back = returned.reshape(total, -1)
    mine = jnp.einsum(
        "gsp,sk->pgk", chosen.astype(jnp.float32), flat_back, precision=lax.Precision.HIGHEST
    )
    mine = pick_columns(
        mine.reshape(local * groups, -1), neighbours.reshape(local * groups, -1)
    ).reshape(local, groups, -1)
    return mine - jnp.mean(mine, axis=2, keepdims=True)


MESH = pl.DeviceIdType.MESH
CHUNKS = 4


def route_kernel(groups, columns, marks_ref, own_ref, out_ref, pool, marks, packed,
                 own_sem, mate_send, mate_recv, mark_send, mark_recv,
                 line_send, line_recv, move_send, move_recv):
    grp = lax.axis_index("grp")
    orient = lax.axis_index("orient")
    place, core = orient // 2, orient % 2
    local = own_ref.shape[0]
    half = own_ref.shape[1] // 2
    span = half // CHUNKS
    rows = out_ref.shape[0] // (groups * columns)
    tile = min(1024, span)

    barrier = pltpu.get_barrier_semaphore()
    for step in range(1, 2 * columns):
        pl.semaphore_signal(barrier, inc=1, device_id=(grp, (orient + step) % (2 * columns)), device_id_type=MESH)
    for step in range(1, groups):
        for side in range(2):
            pl.semaphore_signal(
                barrier, inc=1, device_id=((grp + step) % groups, 2 * place + side), device_id_type=MESH
            )
    pl.semaphore_wait(barrier, 2 * columns - 1 + 2 * (groups - 1))

    def cols(chunk):
        return pl.ds(pl.multiple_of(chunk * span, 128), span)

    def mark_copy(step):
        return pltpu.make_async_remote_copy(
            src_ref=marks_ref, dst_ref=marks.at[orient],
            send_sem=mark_send.at[step], recv_sem=mark_recv.at[orient],
            device_id=(grp, (orient + step) % (2 * columns)), device_id_type=MESH)

    def mark_arrival(source):
        return pltpu.make_async_remote_copy(
            src_ref=marks_ref, dst_ref=marks.at[source],
            send_sem=mark_send.at[0], recv_sem=mark_recv.at[source],
            device_id=(grp, (orient + 1) % (2 * columns)), device_id_type=MESH)

    def own_copy(chunk):
        return pltpu.make_async_copy(
            own_ref.at[:, pl.ds(pl.multiple_of(core * half + chunk * span, 128), span)],
            pool.at[place, pl.ds(pl.multiple_of(core * local, 16), local), cols(chunk)],
            own_sem.at[chunk])

    def mate_copy(chunk):
        return pltpu.make_async_remote_copy(
            src_ref=own_ref.at[:, pl.ds(pl.multiple_of((1 - core) * half + chunk * span, 128), span)],
            dst_ref=pool.at[place, pl.ds(pl.multiple_of(core * local, 16), local), cols(chunk)],
            send_sem=mate_send.at[chunk], recv_sem=mate_recv.at[chunk],
            device_id=(grp, 2 * place + 1 - core), device_id_type=MESH)

    def mate_arrival(chunk):
        return pltpu.make_async_remote_copy(
            src_ref=own_ref.at[:, pl.ds(pl.multiple_of((1 - core) * half + chunk * span, 128), span)],
            dst_ref=pool.at[place, pl.ds(pl.multiple_of((1 - core) * local, 16), local), cols(chunk)],
            send_sem=mate_send.at[chunk], recv_sem=mate_recv.at[chunk],
            device_id=(grp, 2 * place + 1 - core), device_id_type=MESH)

    def line_copy(source, way, chunk):
        to = place + 1 - 2 * way
        return pltpu.make_async_remote_copy(
            src_ref=pool.at[source, :, cols(chunk)], dst_ref=pool.at[source, :, cols(chunk)],
            send_sem=line_send.at[source, way, chunk], recv_sem=line_recv.at[source, chunk],
            device_id=(grp, 2 * to + core), device_id_type=MESH)

    def has_next(way):
        return place < columns - 1 if way == 0 else place > 0

    def move_copy(source, group, side, chunk):
        return pltpu.make_async_remote_copy(
            src_ref=packed.at[source, pl.ds((group * 2 + side) * rows, rows), cols(chunk)],
            dst_ref=out_ref.at[
                pl.ds(pl.multiple_of((grp * columns + source) * rows, 16), rows),
                pl.ds(pl.multiple_of(core * half + chunk * span, 128), span)],
            send_sem=move_send.at[source, group, side, chunk],
            recv_sem=move_recv.at[source, grp, core, chunk],
            device_id=(group, 2 * place + side), device_id_type=MESH)

    def move_arrival(source, group, side, chunk):
        return pltpu.make_async_remote_copy(
            src_ref=packed.at[source, pl.ds(0, rows), cols(chunk)],
            dst_ref=out_ref.at[
                pl.ds(pl.multiple_of((group * columns + source) * rows, 16), rows),
                pl.ds(pl.multiple_of(side * half + chunk * span, 128), span)],
            send_sem=move_send.at[source, group, side, chunk],
            recv_sem=move_recv.at[source, group, side, chunk],
            device_id=(group, 2 * place + side), device_id_type=MESH)

    def stay_copy(source, chunk):
        return pltpu.make_async_copy(
            packed.at[source, pl.ds(pl.multiple_of((grp * 2 + core) * rows, 16), rows), cols(chunk)],
            out_ref.at[
                pl.ds(pl.multiple_of((grp * columns + source) * rows, 16), rows),
                pl.ds(pl.multiple_of(core * half + chunk * span, 128), span)],
            move_recv.at[source, grp, core, chunk])

    for chunk in range(CHUNKS):
        own_copy(chunk).start()
        mate_copy(chunk).start()
    for step in range(1, 2 * columns):
        mark_copy(step).start()
    marks[orient] = marks_ref[...]

    def pack(source, chunk):
        names = jnp.maximum(marks[2 * source], marks[2 * source + 1])[:, : 2 * local]
        want = 2 * rows * place + lax.broadcasted_iota(jnp.int32, (2 * rows, 2 * local), 0)
        select = jnp.concatenate(
            [
                jnp.where(jnp.broadcast_to(names[g : g + 1], want.shape) == want, 1.0, 0.0)
                for g in range(groups)
            ],
            axis=0,
        ).astype(jnp.bfloat16)

        @pl.loop(0, span // tile)
        def _(part):
            at = pl.ds(pl.multiple_of(chunk * span + part * tile, 128), tile)
            packed[source, :, at] = jnp.dot(
                select, pool[source, :, at], preferred_element_type=jnp.float32
            ).astype(jnp.bfloat16)

        for group in range(groups):
            for side in range(2):
                mine = (grp == group) & (core == side)

                @pl.when(mine)
                def _():
                    stay_copy(source, chunk).start()

                @pl.when(jnp.logical_not(mine))
                def _():
                    move_copy(source, group, side, chunk).start()

    @pl.loop(0, CHUNKS)
    def _(chunk):
        own_copy(chunk).wait()
        mate_arrival(chunk).wait_recv()
        for way in range(2):
            @pl.when(has_next(way))
            def _():
                line_copy(place, way, chunk).start()

    for step in range(1, 2 * columns):
        mark_arrival((orient + step) % (2 * columns)).wait_recv()

    @pl.loop(0, CHUNKS)
    def _(chunk):
        pack(place, chunk)

    @pl.loop(1, columns)
    def _(far):
        @pl.loop(0, CHUNKS)
        def _(chunk):
            for way in range(2):
                source = place - far + 2 * far * way

                @pl.when((source >= 0) & (source < columns))
                def _():
                    line_copy(source, way, chunk).wait_recv()

                    @pl.when(has_next(way))
                    def _():
                        line_copy(source, way, chunk).start()

                    pack(source, chunk)

    for step in range(1, 2 * columns):
        mark_copy(step).wait_send()

    @pl.loop(0, CHUNKS)
    def _(chunk):
        mate_copy(chunk).wait_send()

        @pl.loop(0, columns)
        def _(source):
            for way in range(2):
                came = source <= place if way == 0 else source >= place

                @pl.when(came & has_next(way))
                def _():
                    line_copy(source, way, chunk).wait_send()

            for group in range(groups):
                for side in range(2):
                    mine = (grp == group) & (core == side)

                    @pl.when(mine)
                    def _():
                        stay_copy(source, chunk).wait()

                    @pl.when(jnp.logical_not(mine))
                    def _():
                        move_copy(source, group, side, chunk).wait_send()
                        move_arrival(source, group, side, chunk).wait_recv()


def route(marks, payload, groups, columns, rows):
    local, width = payload.shape
    half = width // 2
    dma = pltpu.SemaphoreType.DMA
    return pl.pallas_call(
        functools.partial(route_kernel, groups, columns),
        out_shape=jax.ShapeDtypeStruct((groups * columns * rows, width), payload.dtype),
        in_specs=[pl.BlockSpec(memory_space=pltpu.VMEM), pl.BlockSpec(memory_space=pl.ANY)],
        out_specs=pl.BlockSpec(memory_space=pl.ANY),
        scratch_shapes=[
            pltpu.VMEM((columns, 2 * local, half), jnp.bfloat16),
            pltpu.VMEM((2 * columns,) + marks.shape, jnp.int32),
            pltpu.VMEM((columns, groups * 2 * rows, half), jnp.bfloat16),
            dma((CHUNKS,)), dma((CHUNKS,)), dma((CHUNKS,)),
            dma((2 * columns,)), dma((2 * columns,)),
            dma((columns, 2, CHUNKS)), dma((columns, CHUNKS)),
            dma((columns, groups, 2, CHUNKS)), dma((columns, groups, 2, CHUNKS)),
        ],
        compiler_params=pltpu.CompilerParams(
            collective_id=0, has_side_effects=True, vmem_limit_bytes=48 * 2**20
        ),
    )(marks, payload)


def score_kernel(scale, real_ref, imag_ref, ctf_ref, weight_ref, refs_ref, out_ref):
    ctf = ctf_ref[...].astype(jnp.float32)
    tone = weight_ref[...] * ctf
    power = (tone * ctf).astype(jnp.bfloat16)
    real = (tone * real_ref[...].astype(jnp.float32)).astype(jnp.bfloat16)
    imag = (tone * imag_ref[...].astype(jnp.float32)).astype(jnp.bfloat16)
    ref_real = refs_ref[:, 0, :]
    ref_imag = refs_ref[:, 1, :]
    rr, ri = ref_real.astype(jnp.float32), ref_imag.astype(jnp.float32)
    ref_power = (rr * rr + ri * ri).astype(jnp.bfloat16)
    contract = (((1,), (1,)), ((), ()))
    dot = functools.partial(
        lax.dot_general, dimension_numbers=contract, preferred_element_type=jnp.float32
    )
    step = (dot(power, ref_power) - 2.0 * (dot(real, ref_real) + dot(imag, ref_imag))) * scale

    @pl.when(pl.program_id(0) == 0)
    def _():
        out_ref[...] = jnp.zeros_like(out_ref)

    out_ref[...] += step


def score(arrived, weight, refs, block):
    slots, width = arrived.shape
    pixels = width // 3
    side = pixels // 2 // block
    wide = refs.shape[0]

    def part(which):
        return pl.BlockSpec((slots, block), lambda i: (0, i // side * 3 * side + which * side + i % side))

    return pl.pallas_call(
        functools.partial(score_kernel, 1.0 / math.sqrt(PIX)),
        grid=(pixels // block,),
        out_shape=jax.ShapeDtypeStruct((slots, wide), jnp.float32),
        in_specs=[
            part(0), part(1), part(2),
            pl.BlockSpec((1, block), lambda i: (0, i)),
            pl.BlockSpec((wide, 2, block), lambda i: (0, 0, i)),
        ],
        out_specs=pl.BlockSpec((slots, wide), lambda i: (0, 0)),
        compiler_params=pltpu.CompilerParams(vmem_limit_bytes=48 * 2**20),
    )(arrived, arrived, arrived, weight, refs)


def pick_kernel(slot_ref, table_ref, lists_ref, out_ref, rows_ref):
    count, entries = lists_ref.shape
    wide = table_ref.shape[1]

    @pl.loop(0, count)
    def _(i):
        rows_ref[pl.ds(i, 1), :] = table_ref[pl.ds(slot_ref[i], 1), :]

    lists = lists_ref[...]
    place = lists % entries
    value = jnp.zeros((count, entries), jnp.float32)
    for b in range(wide // entries):
        here = jnp.take_along_axis(rows_ref[:, b * entries : (b + 1) * entries], place, axis=1)
        value = jnp.where(lists // entries == b, here, value)
    out_ref[...] = value - jnp.mean(value, axis=1, keepdims=True)


def pick(slot, table, lists):
    vmem = pl.BlockSpec(memory_space=pltpu.VMEM)
    return pl.pallas_call(
        pick_kernel,
        out_shape=jax.ShapeDtypeStruct(lists.shape, jnp.float32),
        in_specs=[pl.BlockSpec(memory_space=pltpu.SMEM), vmem, vmem],
        out_specs=vmem,
        scratch_shapes=[pltpu.VMEM((lists.shape[0], table.shape[1]), jnp.float32)],
    )(slot, table, lists)


def per_device_routed(images, ctf, shifts, home, neighbours, references, noise_weight):
    groups = lax.axis_size("grp")
    owners = lax.axis_size("orient")
    local, _, pixels = images.shape
    slots = max(2, 2 * local // owners)
    core = lax.axis_index("orient") % 2
    target = home[:, :, 0]
    earlier = jnp.arange(local)[None, :] < jnp.arange(local)[:, None]
    rank = jnp.sum(((target[:, :, None] == target[:, None, :]) & earlier[None]).astype(jnp.int32), axis=2)
    marks = (target * 2 + core) * slots + rank
    lane = jnp.arange(128, dtype=jnp.int32)
    marks = jnp.where(
        (lane // local == core)[None, :], jnp.tile(marks, (1, 128 // local)), -1
    )
    marks = jnp.pad(marks, ((0, -groups % 8), (0, 0)), constant_values=-1)
    cosine, sine = shift_tables(shifts, BOX)
    real = images[:, 0].astype(jnp.float32)
    imag = images[:, 1].astype(jnp.float32)
    cut = (local, 2, pixels // 2)
    payload = jnp.stack(
        [
            (real * cosine - imag * sine).astype(jnp.bfloat16).reshape(cut),
            (real * sine + imag * cosine).astype(jnp.bfloat16).reshape(cut),
            ctf.reshape(cut),
        ],
        axis=2,
    ).reshape(local, 3 * pixels)
    arrived = route(marks, payload, groups, owners // 2, 2 * slots)
    table = score(arrived, noise_weight, references[0], 512)
    returned = lax.all_to_all(
        table.reshape(groups * owners, slots, -1), ("grp", "orient"), split_axis=0, concat_axis=0, tiled=True
    )
    slot = (jnp.arange(groups, dtype=jnp.int32)[:, None] * owners + target) * slots + rank
    entries = neighbours.shape[2]
    return pick(
        slot.T.reshape(-1),
        returned.reshape(groups * owners * slots, -1),
        neighbours.reshape(local * groups, entries),
    ).reshape(neighbours.shape)


def per_device(images, ctf, shifts, home, neighbours, references, noise_weight):
    owners = lax.axis_size("orient")
    local = images.shape[0]
    slots = max(2, 2 * local // owners)
    routed = owners % 2 == 0 and slots % 8 == 0 and local % 16 == 0 and 128 % (2 * local) == 0
    form = per_device_routed if routed else per_device_plain
    return form(images, ctf, shifts, home, neighbours, references, noise_weight)


def solution(mesh):
    in_specs = (
        P(("grp", "orient"), None, None),
        P(("grp", "orient"), None),
        P(("grp", "orient"), None),
        P(None, ("grp", "orient"), None),
        P(("grp", "orient"), None, None),
        P("grp", "orient", None, None),
        P("grp", None),
    )
    out_specs = P(("grp", "orient"), None, None)
    return jax.shard_map(
        per_device, mesh=mesh, in_specs=in_specs, out_specs=out_specs, check_vma=False
    )
```

```python
import functools
import math

import jax
import jax.numpy as jnp
import numpy as np
from jax import lax
from jax.experimental import pallas as pl
from jax.experimental.pallas import tpu as pltpu
from jax.sharding import PartitionSpec as P

BOX = 128
PIX = 8192


def shift_tables(shifts, box):
    half = box // 2
    row = jnp.arange(box, dtype=jnp.int32)
    freq_y = jnp.where(row < half, row, row - box).astype(jnp.float32)
    freq_x = jnp.arange(half, dtype=jnp.int32).astype(jnp.float32)
    grid_y = jnp.broadcast_to(freq_y[:, None], (box, half)).reshape(-1)
    grid_x = jnp.broadcast_to(freq_x[None, :], (box, half)).reshape(-1)
    move_x = shifts[:, 0].astype(jnp.float32)
    move_y = shifts[:, 1].astype(jnp.float32)
    angle = (
        -2.0
        * math.pi
        / box
        * (move_x[:, None] * grid_x[None, :] + move_y[:, None] * grid_y[None, :])
    )
    return (jnp.cos(angle), jnp.sin(angle))


def pick_columns(table, lists):
    width = table.shape[-1]
    marks = (lists[..., None] == jnp.arange(width, dtype=jnp.int32)).astype(jnp.float32)
    return jnp.einsum("ano,ao->an", marks, table, precision=lax.Precision.HIGHEST)


def per_device_plain(images, ctf, shifts, home, neighbours, references, noise_weight):
    groups = home.shape[0]
    owners = lax.axis_size("orient")
    devices = groups * owners
    local = images.shape[0]
    pixels = images.shape[2]
    slots = max(2, 2 * local // owners)
    cosine, sine = shift_tables(shifts, BOX)
    real = images[:, 0].astype(jnp.float32)
    imag = images[:, 1].astype(jnp.float32)
    payload = jnp.stack(
        [real * cosine - imag * sine, real * sine + imag * cosine, ctf.astype(jnp.float32)], axis=1
    ).astype(jnp.bfloat16)
    target = home[:, :, 0]
    places = jnp.arange(owners, dtype=jnp.int32)
    hits = (target[:, :, None] == places[None, None, :]).astype(jnp.int32)
    rank = jnp.sum((jnp.cumsum(hits, axis=1) - hits) * hits, axis=2)
    slot = (jnp.arange(groups, dtype=jnp.int32)[:, None] * owners + target) * slots + rank
    total = devices * slots
    chosen = (slot[:, None, :] == jnp.arange(total, dtype=jnp.int32)[None, :, None]).astype(
        jnp.int32
    )
    select = jnp.sum(chosen, axis=0).astype(jnp.bfloat16)
    buffer = jnp.dot(select, payload.reshape(local, -1), preferred_element_type=jnp.float32).astype(
        jnp.bfloat16
    )
    buffer = buffer.reshape(devices, slots, 3, pixels)
    weight = noise_weight[0]
    blocks = references[0]
    flat_refs = blocks.reshape(blocks.shape[0], -1)
    ref_real = blocks[:, 0].astype(jnp.float32)
    ref_imag = blocks[:, 1].astype(jnp.float32)
    ref_power = (ref_real * ref_real + ref_imag * ref_imag).astype(jnp.bfloat16)
    scale = 1.0 / math.sqrt(PIX)
    contract = (((1,), (1,)), ((), ()))
    arrived = lax.all_to_all(buffer, ("grp", "orient"), split_axis=0, concat_axis=0, tiled=True)
    lead = arrived.shape[:2]
    flat = arrived.reshape(-1, 3, pixels).astype(jnp.float32)
    tone = weight[None, :] * flat[:, 2]
    weighted = (tone[:, None, :] * flat[:, :2]).astype(jnp.bfloat16).reshape(flat.shape[0], -1)
    tone_power = (tone * flat[:, 2]).astype(jnp.bfloat16)
    cross = lax.dot_general(weighted, flat_refs, contract, preferred_element_type=jnp.float32)
    power = lax.dot_general(tone_power, ref_power, contract, preferred_element_type=jnp.float32)
    table = ((power - 2.0 * cross) * scale).reshape(lead + (-1,))
    returned = lax.all_to_all(table, ("grp", "orient"), split_axis=0, concat_axis=0, tiled=True)
    flat_back = returned.reshape(total, -1)
    mine = jnp.einsum(
        "gsp,sk->pgk", chosen.astype(jnp.float32), flat_back, precision=lax.Precision.HIGHEST
    )
    mine = pick_columns(
        mine.reshape(local * groups, -1), neighbours.reshape(local * groups, -1)
    ).reshape(local, groups, -1)
    return mine - jnp.mean(mine, axis=2, keepdims=True)


MESH = pl.DeviceIdType.MESH
CHUNKS = 4


def route_kernel(groups, columns, marks_ref, own_ref, refs_ref, out_ref, flat_ref, pool, marks, packed,
                 raw, flat, raw_sem, flat_sem, own_sem, mate_send, mate_recv, mark_send, mark_recv,
                 line_send, line_recv, move_send, move_recv):
    grp = lax.axis_index("grp")
    orient = lax.axis_index("orient")
    place, core = orient // 2, orient % 2
    local = own_ref.shape[0]
    half = own_ref.shape[1] // 2
    span = half // CHUNKS
    rows = out_ref.shape[0] // (groups * columns)
    tile = min(1024, span)

    barrier = pltpu.get_barrier_semaphore()
    for step in range(1, 2 * columns):
        pl.semaphore_signal(barrier, inc=1, device_id=(grp, (orient + step) % (2 * columns)), device_id_type=MESH)
    for step in range(1, groups):
        for side in range(2):
            pl.semaphore_signal(
                barrier, inc=1, device_id=((grp + step) % groups, 2 * place + side), device_id_type=MESH
            )
    pl.semaphore_wait(barrier, 2 * columns - 1 + 2 * (groups - 1))

    def cols(chunk):
        return pl.ds(pl.multiple_of(chunk * span, 128), span)

    def mark_copy(step):
        return pltpu.make_async_remote_copy(
            src_ref=marks_ref, dst_ref=marks.at[orient],
            send_sem=mark_send.at[step], recv_sem=mark_recv.at[orient],
            device_id=(grp, (orient + step) % (2 * columns)), device_id_type=MESH)

    def mark_arrival(source):
        return pltpu.make_async_remote_copy(
            src_ref=marks_ref, dst_ref=marks.at[source],
            send_sem=mark_send.at[0], recv_sem=mark_recv.at[source],
            device_id=(grp, (orient + 1) % (2 * columns)), device_id_type=MESH)

    def own_copy(chunk):
        return pltpu.make_async_copy(
            own_ref.at[:, pl.ds(pl.multiple_of(core * half + chunk * span, 128), span)],
            pool.at[place, pl.ds(pl.multiple_of(core * local, 16), local), cols(chunk)],
            own_sem.at[chunk])

    def mate_copy(chunk):
        return pltpu.make_async_remote_copy(
            src_ref=own_ref.at[:, pl.ds(pl.multiple_of((1 - core) * half + chunk * span, 128), span)],
            dst_ref=pool.at[place, pl.ds(pl.multiple_of(core * local, 16), local), cols(chunk)],
            send_sem=mate_send.at[chunk], recv_sem=mate_recv.at[chunk],
            device_id=(grp, 2 * place + 1 - core), device_id_type=MESH)

    def mate_arrival(chunk):
        return pltpu.make_async_remote_copy(
            src_ref=own_ref.at[:, pl.ds(pl.multiple_of((1 - core) * half + chunk * span, 128), span)],
            dst_ref=pool.at[place, pl.ds(pl.multiple_of((1 - core) * local, 16), local), cols(chunk)],
            send_sem=mate_send.at[chunk], recv_sem=mate_recv.at[chunk],
            device_id=(grp, 2 * place + 1 - core), device_id_type=MESH)

    def line_copy(source, way, chunk):
        to = place + 1 - 2 * way
        return pltpu.make_async_remote_copy(
            src_ref=pool.at[source, :, cols(chunk)], dst_ref=pool.at[source, :, cols(chunk)],
            send_sem=line_send.at[source, way, chunk], recv_sem=line_recv.at[source, chunk],
            device_id=(grp, 2 * to + core), device_id_type=MESH)

    def has_next(way):
        return place < columns - 1 if way == 0 else place > 0

    def move_copy(source, group, side, chunk):
        return pltpu.make_async_remote_copy(
            src_ref=packed.at[source, pl.ds((group * 2 + side) * rows, rows), cols(chunk)],
            dst_ref=out_ref.at[
                pl.ds(pl.multiple_of((grp * columns + source) * rows, 16), rows),
                pl.ds(pl.multiple_of(core * half + chunk * span, 128), span)],
            send_sem=move_send.at[source, group, side, chunk],
            recv_sem=move_recv.at[source, grp, core, chunk],
            device_id=(group, 2 * place + side), device_id_type=MESH)

    def move_arrival(source, group, side, chunk):
        return pltpu.make_async_remote_copy(
            src_ref=packed.at[source, pl.ds(0, rows), cols(chunk)],
            dst_ref=out_ref.at[
                pl.ds(pl.multiple_of((group * columns + source) * rows, 16), rows),
                pl.ds(pl.multiple_of(side * half + chunk * span, 128), span)],
            send_sem=move_send.at[source, group, side, chunk],
            recv_sem=move_recv.at[source, group, side, chunk],
            device_id=(group, 2 * place + side), device_id_type=MESH)

    def stay_copy(source, chunk):
        return pltpu.make_async_copy(
            packed.at[source, pl.ds(pl.multiple_of((grp * 2 + core) * rows, 16), rows), cols(chunk)],
            out_ref.at[
                pl.ds(pl.multiple_of((grp * columns + source) * rows, 16), rows),
                pl.ds(pl.multiple_of(core * half + chunk * span, 128), span)],
            move_recv.at[source, grp, core, chunk])

    wide, block = flat.shape[2:]
    tiles = refs_ref.shape[2] // block
    first = tiles - (columns - 1) * CHUNKS

    def raw_copy(t):
        at = pl.ds(pl.multiple_of(t * block, 128), block)
        return pltpu.make_async_copy(refs_ref.at[:, :, at], raw.at[t % 2], raw_sem.at[t % 2])

    def flat_copy(t, which):
        at = pl.ds(pl.multiple_of((which * tiles + t) * block, 128), block)
        return pltpu.make_async_copy(flat.at[t % 2, which], flat_ref.at[:, at], flat_sem.at[t % 2, which])

    def lay_out(t):
        raw_copy(t).wait()

        @pl.when(t + 1 < tiles)
        def _():
            raw_copy(t + 1).start()

        @pl.when(t >= 2)
        def _():
            for which in range(3):
                flat_copy(t - 2, which).wait()

        @pl.loop(0, wide // 32)
        def _(r):
            at = pl.ds(pl.multiple_of(r * 32, 32), 32)
            real = raw[t % 2, at, 0, :]
            imag = raw[t % 2, at, 1, :]
            rf, mf = real.astype(jnp.float32), imag.astype(jnp.float32)
            flat[t % 2, 0, at, :] = real
            flat[t % 2, 1, at, :] = imag
            flat[t % 2, 2, at, :] = (rf * rf + mf * mf).astype(jnp.bfloat16)

        for which in range(3):
            flat_copy(t, which).start()

    for chunk in range(CHUNKS):
        own_copy(chunk).start()
        mate_copy(chunk).start()
    raw_copy(0).start()
    for step in range(1, 2 * columns):
        mark_copy(step).start()
    marks[orient] = marks_ref[...]

    def pack(source, chunk):
        names = jnp.maximum(marks[2 * source], marks[2 * source + 1])[:, : 2 * local]
        want = 2 * rows * place + lax.broadcasted_iota(jnp.int32, (2 * rows, 2 * local), 0)
        select = jnp.concatenate(
            [
                jnp.where(jnp.broadcast_to(names[g : g + 1], want.shape) == want, 1.0, 0.0)
                for g in range(groups)
            ],
            axis=0,
        ).astype(jnp.bfloat16)

        @pl.loop(0, span // tile)
        def _(part):
            at = pl.ds(pl.multiple_of(chunk * span + part * tile, 128), tile)
            packed[source, :, at] = jnp.dot(
                select, pool[source, :, at], preferred_element_type=jnp.float32
            ).astype(jnp.bfloat16)

        for group in range(groups):
            for side in range(2):
                mine = (grp == group) & (core == side)

                @pl.when(mine)
                def _():
                    stay_copy(source, chunk).start()

                @pl.when(jnp.logical_not(mine))
                def _():
                    move_copy(source, group, side, chunk).start()

    @pl.loop(0, CHUNKS)
    def _(chunk):
        own_copy(chunk).wait()
        mate_arrival(chunk).wait_recv()
        for way in range(2):
            @pl.when(has_next(way))
            def _():
                line_copy(place, way, chunk).start()

    for step in range(1, 2 * columns):
        mark_arrival((orient + step) % (2 * columns)).wait_recv()

    @pl.loop(0, CHUNKS)
    def _(chunk):
        pack(place, chunk)

    @pl.loop(0, first)
    def _(t):
        lay_out(t)

    @pl.loop(1, columns)
    def _(far):
        @pl.loop(0, CHUNKS)
        def _(chunk):
            for way in range(2):
                source = place - far + 2 * far * way

                @pl.when((source >= 0) & (source < columns))
                def _():
                    line_copy(source, way, chunk).wait_recv()

                    @pl.when(has_next(way))
                    def _():
                        line_copy(source, way, chunk).start()

                    pack(source, chunk)

            lay_out(first + (far - 1) * CHUNKS + chunk)

    for t in (tiles - 2, tiles - 1):
        for which in range(3):
            flat_copy(t, which).wait()

    for step in range(1, 2 * columns):
        mark_copy(step).wait_send()

    @pl.loop(0, CHUNKS)
    def _(chunk):
        mate_copy(chunk).wait_send()

        @pl.loop(0, columns)
        def _(source):
            for way in range(2):
                came = source <= place if way == 0 else source >= place

                @pl.when(came & has_next(way))
                def _():
                    line_copy(source, way, chunk).wait_send()

            for group in range(groups):
                for side in range(2):
                    mine = (grp == group) & (core == side)

                    @pl.when(mine)
                    def _():
                        stay_copy(source, chunk).wait()

                    @pl.when(jnp.logical_not(mine))
                    def _():
                        move_copy(source, group, side, chunk).wait_send()
                        move_arrival(source, group, side, chunk).wait_recv()


def shift_kernel(shifts_ref, turn_ref, images_ref, ctf_ref, out_ref):
    local, pixels = ctf_ref.shape
    half = pixels // 2
    lanes = turn_ref.shape[1]
    side = BOX // 2
    cosine = jnp.broadcast_to(turn_ref[0:1], (local, lanes))
    sine = jnp.broadcast_to(turn_ref[1:2], (local, lanes))
    move_x, move_y = shifts_ref[:, 0:1], shifts_ref[:, 1:2]
    lane = lax.broadcasted_iota(jnp.int32, (local, lanes), 1)
    base = move_x * (lane % side) + move_y * (lane // side)

    @pl.loop(0, pixels // lanes)
    def _(piece):
        at = pl.ds(pl.multiple_of(piece * lanes, lanes), lanes)
        steps = (base + move_y * (piece * (lanes // side))) & (BOX - 1)
        c = jnp.take_along_axis(cosine, steps, axis=1)
        s = jnp.take_along_axis(sine, steps, axis=1)
        real = images_ref[:, 0, at].astype(jnp.float32)
        imag = images_ref[:, 1, at].astype(jnp.float32)
        start = piece * lanes + piece // (half // lanes) * 2 * half

        def put(which, value):
            to = pl.ds(pl.multiple_of(start + which * half, lanes), lanes)
            out_ref[:, to] = value

        put(0, (real * c - imag * s).astype(jnp.bfloat16))
        put(1, (real * s + imag * c).astype(jnp.bfloat16))
        put(2, ctf_ref[:, at])


def shift(images, ctf, shifts):
    local, _, pixels = images.shape
    angle = -2.0 * np.pi / BOX * np.arange(BOX)
    turn = np.zeros((8, BOX), np.float32)
    turn[0], turn[1] = np.cos(angle), np.sin(angle)
    vmem = pl.BlockSpec(memory_space=pltpu.VMEM)
    return pl.pallas_call(
        shift_kernel,
        out_shape=jax.ShapeDtypeStruct((local, 3 * pixels), jnp.bfloat16),
        in_specs=[vmem] * 4,
        out_specs=vmem,
        compiler_params=pltpu.CompilerParams(vmem_limit_bytes=32 * 2**20),
    )(shifts, jnp.asarray(turn), images, ctf)


def route(marks, payload, refs, groups, columns, rows):
    local, width = payload.shape
    wide, _, pixels = refs.shape
    block = 512
    half = width // 2
    dma = pltpu.SemaphoreType.DMA
    return pl.pallas_call(
        functools.partial(route_kernel, groups, columns),
        out_shape=(
            jax.ShapeDtypeStruct((groups * columns * rows, width), payload.dtype),
            jax.ShapeDtypeStruct((wide, 3 * pixels), refs.dtype),
        ),
        in_specs=[pl.BlockSpec(memory_space=pltpu.VMEM)] + [pl.BlockSpec(memory_space=pl.ANY)] * 2,
        out_specs=(pl.BlockSpec(memory_space=pl.ANY), pl.BlockSpec(memory_space=pl.ANY)),
        scratch_shapes=[
            pltpu.VMEM((columns, 2 * local, half), jnp.bfloat16),
            pltpu.VMEM((2 * columns,) + marks.shape, jnp.int32),
            pltpu.VMEM((columns, groups * 2 * rows, half), jnp.bfloat16),
            pltpu.VMEM((2, wide, 2, block), refs.dtype),
            pltpu.VMEM((2, 3, wide, block), refs.dtype),
            dma((2,)), dma((2, 3)),
            dma((CHUNKS,)), dma((CHUNKS,)), dma((CHUNKS,)),
            dma((2 * columns,)), dma((2 * columns,)),
            dma((columns, 2, CHUNKS)), dma((columns, CHUNKS)),
            dma((columns, groups, 2, CHUNKS)), dma((columns, groups, 2, CHUNKS)),
        ],
        compiler_params=pltpu.CompilerParams(
            collective_id=0, has_side_effects=True, vmem_limit_bytes=48 * 2**20
        ),
    )(marks, payload, refs)


def score_kernel(scale, real_ref, imag_ref, ctf_ref, weight_ref, ref_real, ref_imag, ref_power, out_ref):
    ctf = ctf_ref[...].astype(jnp.float32)
    tone = weight_ref[...] * ctf
    power = (tone * ctf).astype(jnp.bfloat16)
    real = (tone * real_ref[...].astype(jnp.float32)).astype(jnp.bfloat16)
    imag = (tone * imag_ref[...].astype(jnp.float32)).astype(jnp.bfloat16)
    contract = (((1,), (1,)), ((), ()))
    dot = functools.partial(
        lax.dot_general, dimension_numbers=contract, preferred_element_type=jnp.float32
    )
    step = (
        dot(power, ref_power[...]) - 2.0 * (dot(real, ref_real[...]) + dot(imag, ref_imag[...]))
    ) * scale

    @pl.when(pl.program_id(0) == 0)
    def _():
        out_ref[...] = jnp.zeros_like(out_ref)

    out_ref[...] += step


def score(arrived, weight, refs, block):
    slots, width = arrived.shape
    pixels = width // 3
    side = pixels // 2 // block
    wide = refs.shape[0]

    def part(which):
        return pl.BlockSpec((slots, block), lambda i: (0, i // side * 3 * side + which * side + i % side))

    def known(which):
        return pl.BlockSpec((wide, block), lambda i: (0, which * 2 * side + i))

    return pl.pallas_call(
        functools.partial(score_kernel, 1.0 / math.sqrt(PIX)),
        grid=(pixels // block,),
        out_shape=jax.ShapeDtypeStruct((slots, wide), jnp.float32),
        in_specs=[
            part(0), part(1), part(2),
            pl.BlockSpec((1, block), lambda i: (0, i)),
            known(0), known(1), known(2),
        ],
        out_specs=pl.BlockSpec((slots, wide), lambda i: (0, 0)),
        compiler_params=pltpu.CompilerParams(vmem_limit_bytes=48 * 2**20),
    )(arrived, arrived, arrived, weight, refs, refs, refs)


def pick_kernel(slot_ref, table_ref, lists_ref, out_ref, rows_ref):
    count, entries = lists_ref.shape
    wide = table_ref.shape[1]

    @pl.loop(0, count)
    def _(i):
        rows_ref[pl.ds(i, 1), :] = table_ref[pl.ds(slot_ref[i], 1), :]

    lists = lists_ref[...]
    place = lists % entries
    value = jnp.zeros((count, entries), jnp.float32)
    for b in range(wide // entries):
        here = jnp.take_along_axis(rows_ref[:, b * entries : (b + 1) * entries], place, axis=1)
        value = jnp.where(lists // entries == b, here, value)
    out_ref[...] = value - jnp.mean(value, axis=1, keepdims=True)


def pick(slot, table, lists):
    vmem = pl.BlockSpec(memory_space=pltpu.VMEM)
    return pl.pallas_call(
        pick_kernel,
        out_shape=jax.ShapeDtypeStruct(lists.shape, jnp.float32),
        in_specs=[pl.BlockSpec(memory_space=pltpu.SMEM), vmem, vmem],
        out_specs=vmem,
        scratch_shapes=[pltpu.VMEM((lists.shape[0], table.shape[1]), jnp.float32)],
    )(slot, table, lists)


def per_device_routed(images, ctf, shifts, home, neighbours, references, noise_weight):
    groups = lax.axis_size("grp")
    owners = lax.axis_size("orient")
    local, _, pixels = images.shape
    slots = max(2, 2 * local // owners)
    core = lax.axis_index("orient") % 2
    target = home[:, :, 0]
    earlier = jnp.arange(local)[None, :] < jnp.arange(local)[:, None]
    rank = jnp.sum(((target[:, :, None] == target[:, None, :]) & earlier[None]).astype(jnp.int32), axis=2)
    marks = (target * 2 + core) * slots + rank
    lane = jnp.arange(128, dtype=jnp.int32)
    marks = jnp.where(
        (lane // local == core)[None, :], jnp.tile(marks, (1, 128 // local)), -1
    )
    marks = jnp.pad(marks, ((0, -groups % 8), (0, 0)), constant_values=-1)
    payload = shift(images, ctf, shifts)
    arrived, flat = route(marks, payload, references[0], groups, owners // 2, 2 * slots)
    table = score(arrived, noise_weight, flat, 1024)
    returned = lax.all_to_all(
        table.reshape(groups * owners, slots, -1), ("grp", "orient"), split_axis=0, concat_axis=0, tiled=True
    )
    slot = (jnp.arange(groups, dtype=jnp.int32)[:, None] * owners + target) * slots + rank
    entries = neighbours.shape[2]
    return pick(
        slot.T.reshape(-1),
        returned.reshape(groups * owners * slots, -1),
        neighbours.reshape(local * groups, entries),
    ).reshape(neighbours.shape)


def per_device(images, ctf, shifts, home, neighbours, references, noise_weight):
    owners = lax.axis_size("orient")
    local = images.shape[0]
    slots = max(2, 2 * local // owners)
    parts = images.shape[2] // 512
    long = parts >= (owners // 2 - 1) * CHUNKS and images.shape[2] % 2048 == 0
    routed = long and owners % 2 == 0 and slots % 8 == 0 and local % 16 == 0 and 128 % (2 * local) == 0
    form = per_device_routed if routed else per_device_plain
    return form(images, ctf, shifts, home, neighbours, references, noise_weight)


def solution(mesh):
    in_specs = (
        P(("grp", "orient"), None, None),
        P(("grp", "orient"), None),
        P(("grp", "orient"), None),
        P(None, ("grp", "orient"), None),
        P(("grp", "orient"), None, None),
        P("grp", "orient", None, None),
        P("grp", None),
    )
    out_specs = P(("grp", "orient"), None, None)
    return jax.shard_map(
        per_device, mesh=mesh, in_specs=in_specs, out_specs=out_specs, check_vma=False
    )
```

```python
import functools
import math

import jax
import jax.numpy as jnp
import numpy as np
from jax import lax
from jax.experimental import pallas as pl
from jax.experimental.pallas import tpu as pltpu
from jax.sharding import PartitionSpec as P

BOX = 128
PIX = 8192


def shift_tables(shifts, box):
    half = box // 2
    row = jnp.arange(box, dtype=jnp.int32)
    freq_y = jnp.where(row < half, row, row - box).astype(jnp.float32)
    freq_x = jnp.arange(half, dtype=jnp.int32).astype(jnp.float32)
    grid_y = jnp.broadcast_to(freq_y[:, None], (box, half)).reshape(-1)
    grid_x = jnp.broadcast_to(freq_x[None, :], (box, half)).reshape(-1)
    move_x = shifts[:, 0].astype(jnp.float32)
    move_y = shifts[:, 1].astype(jnp.float32)
    angle = (
        -2.0
        * math.pi
        / box
        * (move_x[:, None] * grid_x[None, :] + move_y[:, None] * grid_y[None, :])
    )
    return (jnp.cos(angle), jnp.sin(angle))


def pick_columns(table, lists):
    width = table.shape[-1]
    marks = (lists[..., None] == jnp.arange(width, dtype=jnp.int32)).astype(jnp.float32)
    return jnp.einsum("ano,ao->an", marks, table, precision=lax.Precision.HIGHEST)


def per_device_plain(images, ctf, shifts, home, neighbours, references, noise_weight):
    groups = home.shape[0]
    owners = lax.axis_size("orient")
    devices = groups * owners
    local = images.shape[0]
    pixels = images.shape[2]
    slots = max(2, 2 * local // owners)
    cosine, sine = shift_tables(shifts, BOX)
    real = images[:, 0].astype(jnp.float32)
    imag = images[:, 1].astype(jnp.float32)
    payload = jnp.stack(
        [real * cosine - imag * sine, real * sine + imag * cosine, ctf.astype(jnp.float32)], axis=1
    ).astype(jnp.bfloat16)
    target = home[:, :, 0]
    places = jnp.arange(owners, dtype=jnp.int32)
    hits = (target[:, :, None] == places[None, None, :]).astype(jnp.int32)
    rank = jnp.sum((jnp.cumsum(hits, axis=1) - hits) * hits, axis=2)
    slot = (jnp.arange(groups, dtype=jnp.int32)[:, None] * owners + target) * slots + rank
    total = devices * slots
    chosen = (slot[:, None, :] == jnp.arange(total, dtype=jnp.int32)[None, :, None]).astype(
        jnp.int32
    )
    select = jnp.sum(chosen, axis=0).astype(jnp.bfloat16)
    buffer = jnp.dot(select, payload.reshape(local, -1), preferred_element_type=jnp.float32).astype(
        jnp.bfloat16
    )
    buffer = buffer.reshape(devices, slots, 3, pixels)
    weight = noise_weight[0]
    blocks = references[0]
    flat_refs = blocks.reshape(blocks.shape[0], -1)
    ref_real = blocks[:, 0].astype(jnp.float32)
    ref_imag = blocks[:, 1].astype(jnp.float32)
    ref_power = (ref_real * ref_real + ref_imag * ref_imag).astype(jnp.bfloat16)
    scale = 1.0 / math.sqrt(PIX)
    contract = (((1,), (1,)), ((), ()))
    arrived = lax.all_to_all(buffer, ("grp", "orient"), split_axis=0, concat_axis=0, tiled=True)
    lead = arrived.shape[:2]
    flat = arrived.reshape(-1, 3, pixels).astype(jnp.float32)
    tone = weight[None, :] * flat[:, 2]
    weighted = (tone[:, None, :] * flat[:, :2]).astype(jnp.bfloat16).reshape(flat.shape[0], -1)
    tone_power = (tone * flat[:, 2]).astype(jnp.bfloat16)
    cross = lax.dot_general(weighted, flat_refs, contract, preferred_element_type=jnp.float32)
    power = lax.dot_general(tone_power, ref_power, contract, preferred_element_type=jnp.float32)
    table = ((power - 2.0 * cross) * scale).reshape(lead + (-1,))
    returned = lax.all_to_all(table, ("grp", "orient"), split_axis=0, concat_axis=0, tiled=True)
    flat_back = returned.reshape(total, -1)
    mine = jnp.einsum(
        "gsp,sk->pgk", chosen.astype(jnp.float32), flat_back, precision=lax.Precision.HIGHEST
    )
    mine = pick_columns(
        mine.reshape(local * groups, -1), neighbours.reshape(local * groups, -1)
    ).reshape(local, groups, -1)
    return mine - jnp.mean(mine, axis=2, keepdims=True)


MESH = pl.DeviceIdType.MESH
CHUNKS = 4


def route_kernel(groups, columns, marks_ref, own_ref, refs_ref, out_ref, flat_ref, pool, marks, packed,
                 raw, flat, raw_sem, flat_sem, own_sem, mate_send, mate_recv, mark_send, mark_recv,
                 line_send, line_recv, move_send, move_recv):
    grp = lax.axis_index("grp")
    orient = lax.axis_index("orient")
    place, core = orient // 2, orient % 2
    local = own_ref.shape[0]
    half = own_ref.shape[1] // 2
    span = half // CHUNKS
    rows = out_ref.shape[0] // (groups * columns)
    tile = min(1024, span)

    barrier = pltpu.get_barrier_semaphore()
    for step in range(1, 2 * columns):
        pl.semaphore_signal(barrier, inc=1, device_id=(grp, (orient + step) % (2 * columns)), device_id_type=MESH)
    for step in range(1, groups):
        for side in range(2):
            pl.semaphore_signal(
                barrier, inc=1, device_id=((grp + step) % groups, 2 * place + side), device_id_type=MESH
            )
    pl.semaphore_wait(barrier, 2 * columns - 1 + 2 * (groups - 1))

    def cols(chunk):
        return pl.ds(pl.multiple_of(chunk * span, 128), span)

    def mark_copy(step):
        return pltpu.make_async_remote_copy(
            src_ref=marks_ref, dst_ref=marks.at[orient],
            send_sem=mark_send.at[step], recv_sem=mark_recv.at[orient],
            device_id=(grp, (orient + step) % (2 * columns)), device_id_type=MESH)

    def mark_arrival(source):
        return pltpu.make_async_remote_copy(
            src_ref=marks_ref, dst_ref=marks.at[source],
            send_sem=mark_send.at[0], recv_sem=mark_recv.at[source],
            device_id=(grp, (orient + 1) % (2 * columns)), device_id_type=MESH)

    def own_copy(chunk):
        return pltpu.make_async_copy(
            own_ref.at[:, pl.ds(pl.multiple_of(core * half + chunk * span, 128), span)],
            pool.at[place, pl.ds(pl.multiple_of(core * local, 16), local), cols(chunk)],
            own_sem.at[chunk])

    def mate_copy(chunk):
        return pltpu.make_async_remote_copy(
            src_ref=own_ref.at[:, pl.ds(pl.multiple_of((1 - core) * half + chunk * span, 128), span)],
            dst_ref=pool.at[place, pl.ds(pl.multiple_of(core * local, 16), local), cols(chunk)],
            send_sem=mate_send.at[chunk], recv_sem=mate_recv.at[chunk],
            device_id=(grp, 2 * place + 1 - core), device_id_type=MESH)

    def mate_arrival(chunk):
        return pltpu.make_async_remote_copy(
            src_ref=own_ref.at[:, pl.ds(pl.multiple_of((1 - core) * half + chunk * span, 128), span)],
            dst_ref=pool.at[place, pl.ds(pl.multiple_of((1 - core) * local, 16), local), cols(chunk)],
            send_sem=mate_send.at[chunk], recv_sem=mate_recv.at[chunk],
            device_id=(grp, 2 * place + 1 - core), device_id_type=MESH)

    def line_copy(source, way, chunk):
        to = place + 1 - 2 * way
        return pltpu.make_async_remote_copy(
            src_ref=pool.at[source, :, cols(chunk)], dst_ref=pool.at[source, :, cols(chunk)],
            send_sem=line_send.at[source, way, chunk], recv_sem=line_recv.at[source, chunk],
            device_id=(grp, 2 * to + core), device_id_type=MESH)

    def has_next(way):
        return place < columns - 1 if way == 0 else place > 0

    def move_copy(source, group, side, chunk):
        return pltpu.make_async_remote_copy(
            src_ref=packed.at[source, pl.ds(pl.multiple_of((group * 2 + side) * rows, 16), rows), cols(chunk)],
            dst_ref=out_ref.at[
                pl.ds(pl.multiple_of((grp * columns + source) * rows, 16), rows),
                pl.ds(pl.multiple_of(core * half + chunk * span, 128), span)],
            send_sem=move_send.at[source, group, side, chunk],
            recv_sem=move_recv.at[source, grp, core, chunk],
            device_id=(group, 2 * place + side), device_id_type=MESH)

    def move_arrival(source, group, side, chunk):
        return pltpu.make_async_remote_copy(
            src_ref=packed.at[source, pl.ds(0, rows), cols(chunk)],
            dst_ref=out_ref.at[
                pl.ds(pl.multiple_of((group * columns + source) * rows, 16), rows),
                pl.ds(pl.multiple_of(side * half + chunk * span, 128), span)],
            send_sem=move_send.at[source, group, side, chunk],
            recv_sem=move_recv.at[source, group, side, chunk],
            device_id=(group, 2 * place + side), device_id_type=MESH)

    def stay_copy(source, chunk):
        return pltpu.make_async_copy(
            packed.at[source, pl.ds(pl.multiple_of((grp * 2 + core) * rows, 16), rows), cols(chunk)],
            out_ref.at[
                pl.ds(pl.multiple_of((grp * columns + source) * rows, 16), rows),
                pl.ds(pl.multiple_of(core * half + chunk * span, 128), span)],
            move_recv.at[source, grp, core, chunk])

    wide, block = flat.shape[2:]
    tiles = refs_ref.shape[2] // block
    first = tiles - (columns - 1) * CHUNKS

    def raw_copy(t):
        at = pl.ds(pl.multiple_of(t * block, 128), block)
        return pltpu.make_async_copy(refs_ref.at[:, :, at], raw.at[t % 2], raw_sem.at[t % 2])

    def flat_copy(t, which):
        at = pl.ds(pl.multiple_of((which * tiles + t) * block, 128), block)
        return pltpu.make_async_copy(flat.at[t % 2, which], flat_ref.at[:, at], flat_sem.at[t % 2, which])

    def lay_out(t):
        raw_copy(t).wait()

        @pl.when(t + 1 < tiles)
        def _():
            raw_copy(t + 1).start()

        @pl.when(t >= 2)
        def _():
            for which in range(3):
                flat_copy(t - 2, which).wait()

        @pl.loop(0, wide // 32)
        def _(r):
            at = pl.ds(pl.multiple_of(r * 32, 32), 32)
            real = raw[t % 2, at, 0, :]
            imag = raw[t % 2, at, 1, :]
            rf, mf = real.astype(jnp.float32), imag.astype(jnp.float32)
            flat[t % 2, 0, at, :] = real
            flat[t % 2, 1, at, :] = imag
            flat[t % 2, 2, at, :] = (rf * rf + mf * mf).astype(jnp.bfloat16)

        for which in range(3):
            flat_copy(t, which).start()

    for chunk in range(CHUNKS):
        own_copy(chunk).start()
        mate_copy(chunk).start()
    raw_copy(0).start()
    for step in range(1, 2 * columns):
        mark_copy(step).start()
    marks[orient] = marks_ref[...]

    def pack(source, chunk):
        names = jnp.maximum(marks[2 * source], marks[2 * source + 1])[:, : 2 * local]
        want = 2 * rows * place + lax.broadcasted_iota(jnp.int32, (2 * rows, 2 * local), 0)
        select = jnp.concatenate(
            [
                jnp.where(jnp.broadcast_to(names[g : g + 1], want.shape) == want, 1.0, 0.0)
                for g in range(groups)
            ],
            axis=0,
        ).astype(jnp.bfloat16)

        @pl.loop(0, span // tile)
        def _(part):
            at = pl.ds(pl.multiple_of(chunk * span + part * tile, 128), tile)
            packed[source, :, at] = jnp.dot(
                select, pool[source, :, at], preferred_element_type=jnp.float32
            ).astype(jnp.bfloat16)

        for step in list(range(1, groups, 2)) + list(range(2, groups, 2)):
            for side in range(2):
                move_copy(source, (grp + step) % groups, side, chunk).start()
        move_copy(source, grp, 1 - core, chunk).start()
        stay_copy(source, chunk).start()

    @pl.loop(0, CHUNKS)
    def _(chunk):
        own_copy(chunk).wait()
        mate_arrival(chunk).wait_recv()
        for way in range(2):
            @pl.when(has_next(way))
            def _():
                line_copy(place, way, chunk).start()

    for step in range(1, 2 * columns):
        mark_arrival((orient + step) % (2 * columns)).wait_recv()

    @pl.loop(0, CHUNKS)
    def _(chunk):
        pack(place, chunk)

    @pl.loop(0, first)
    def _(t):
        lay_out(t)

    @pl.loop(1, columns)
    def _(far):
        @pl.loop(0, CHUNKS)
        def _(chunk):
            for way in range(2):
                source = place - far + 2 * far * way

                @pl.when((source >= 0) & (source < columns))
                def _():
                    line_copy(source, way, chunk).wait_recv()

                    @pl.when(has_next(way))
                    def _():
                        line_copy(source, way, chunk).start()

                    pack(source, chunk)

            lay_out(first + (far - 1) * CHUNKS + chunk)

    for t in (tiles - 2, tiles - 1):
        for which in range(3):
            flat_copy(t, which).wait()

    for step in range(1, 2 * columns):
        mark_copy(step).wait_send()

    @pl.loop(0, CHUNKS)
    def _(chunk):
        mate_copy(chunk).wait_send()

        @pl.loop(0, columns)
        def _(source):
            for way in range(2):
                came = source <= place if way == 0 else source >= place

                @pl.when(came & has_next(way))
                def _():
                    line_copy(source, way, chunk).wait_send()

            for group in range(groups):
                for side in range(2):
                    mine = (grp == group) & (core == side)

                    @pl.when(mine)
                    def _():
                        stay_copy(source, chunk).wait()

                    @pl.when(jnp.logical_not(mine))
                    def _():
                        move_copy(source, group, side, chunk).wait_send()
                        move_arrival(source, group, side, chunk).wait_recv()


def shift_kernel(shifts_ref, turn_ref, images_ref, ctf_ref, out_ref):
    local, pixels = ctf_ref.shape
    half = pixels // 2
    lanes = turn_ref.shape[1]
    side = BOX // 2
    cosine = jnp.broadcast_to(turn_ref[0:1], (local, lanes))
    sine = jnp.broadcast_to(turn_ref[1:2], (local, lanes))
    move_x, move_y = shifts_ref[:, 0:1], shifts_ref[:, 1:2]
    lane = lax.broadcasted_iota(jnp.int32, (local, lanes), 1)
    base = move_x * (lane % side) + move_y * (lane // side)

    @pl.loop(0, pixels // lanes, unroll=8)
    def _(piece):
        at = pl.ds(pl.multiple_of(piece * lanes, lanes), lanes)
        steps = (base + move_y * (piece * (lanes // side))) & (BOX - 1)
        c = jnp.take_along_axis(cosine, steps, axis=1)
        s = jnp.take_along_axis(sine, steps, axis=1)
        real = images_ref[:, 0, at].astype(jnp.float32)
        imag = images_ref[:, 1, at].astype(jnp.float32)
        start = piece * lanes + piece // (half // lanes) * 2 * half

        def put(which, value):
            to = pl.ds(pl.multiple_of(start + which * half, lanes), lanes)
            out_ref[:, to] = value

        put(0, (real * c - imag * s).astype(jnp.bfloat16))
        put(1, (real * s + imag * c).astype(jnp.bfloat16))
        put(2, ctf_ref[:, at])


def shift(images, ctf, shifts):
    local, _, pixels = images.shape
    angle = -2.0 * np.pi / BOX * np.arange(BOX)
    turn = np.zeros((8, BOX), np.float32)
    turn[0], turn[1] = np.cos(angle), np.sin(angle)
    vmem = pl.BlockSpec(memory_space=pltpu.VMEM)
    return pl.pallas_call(
        shift_kernel,
        out_shape=jax.ShapeDtypeStruct((local, 3 * pixels), jnp.bfloat16),
        in_specs=[vmem] * 4,
        out_specs=vmem,
        compiler_params=pltpu.CompilerParams(vmem_limit_bytes=32 * 2**20),
    )(shifts, jnp.asarray(turn), images, ctf)


def route(marks, payload, refs, groups, columns, rows):
    local, width = payload.shape
    wide, _, pixels = refs.shape
    block = 512
    half = width // 2
    dma = pltpu.SemaphoreType.DMA
    return pl.pallas_call(
        functools.partial(route_kernel, groups, columns),
        out_shape=(
            jax.ShapeDtypeStruct((groups * columns * rows, width), payload.dtype),
            jax.ShapeDtypeStruct((wide, 3 * pixels), refs.dtype),
        ),
        in_specs=[pl.BlockSpec(memory_space=pltpu.VMEM)] + [pl.BlockSpec(memory_space=pl.ANY)] * 2,
        out_specs=(pl.BlockSpec(memory_space=pl.ANY), pl.BlockSpec(memory_space=pl.ANY)),
        scratch_shapes=[
            pltpu.VMEM((columns, 2 * local, half), jnp.bfloat16),
            pltpu.VMEM((2 * columns,) + marks.shape, jnp.int32),
            pltpu.VMEM((columns, groups * 2 * rows, half), jnp.bfloat16),
            pltpu.VMEM((2, wide, 2, block), refs.dtype),
            pltpu.VMEM((2, 3, wide, block), refs.dtype),
            dma((2,)), dma((2, 3)),
            dma((CHUNKS,)), dma((CHUNKS,)), dma((CHUNKS,)),
            dma((2 * columns,)), dma((2 * columns,)),
            dma((columns, 2, CHUNKS)), dma((columns, CHUNKS)),
            dma((columns, groups, 2, CHUNKS)), dma((columns, groups, 2, CHUNKS)),
        ],
        compiler_params=pltpu.CompilerParams(
            collective_id=0, has_side_effects=True, vmem_limit_bytes=48 * 2**20
        ),
    )(marks, payload, refs)


def score_kernel(scale, real_ref, imag_ref, ctf_ref, weight_ref, ref_real, ref_imag, ref_power, out_ref):
    ctf = ctf_ref[...].astype(jnp.float32)
    tone = weight_ref[...] * ctf
    power = (tone * ctf).astype(jnp.bfloat16)
    real = (tone * real_ref[...].astype(jnp.float32)).astype(jnp.bfloat16)
    imag = (tone * imag_ref[...].astype(jnp.float32)).astype(jnp.bfloat16)
    contract = (((1,), (1,)), ((), ()))
    dot = functools.partial(
        lax.dot_general, dimension_numbers=contract, preferred_element_type=jnp.float32
    )
    step = (
        dot(power, ref_power[...]) - 2.0 * (dot(real, ref_real[...]) + dot(imag, ref_imag[...]))
    ) * scale

    @pl.when(pl.program_id(0) == 0)
    def _():
        out_ref[...] = jnp.zeros_like(out_ref)

    out_ref[...] += step


def score(arrived, weight, refs, block):
    slots, width = arrived.shape
    pixels = width // 3
    side = pixels // 2 // block
    wide = refs.shape[0]

    def part(which):
        return pl.BlockSpec((slots, block), lambda i: (0, i // side * 3 * side + which * side + i % side))

    def known(which):
        return pl.BlockSpec((wide, block), lambda i: (0, which * 2 * side + i))

    return pl.pallas_call(
        functools.partial(score_kernel, 1.0 / math.sqrt(PIX)),
        grid=(pixels // block,),
        out_shape=jax.ShapeDtypeStruct((slots, wide), jnp.float32),
        in_specs=[
            part(0), part(1), part(2),
            pl.BlockSpec((1, block), lambda i: (0, i)),
            known(0), known(1), known(2),
        ],
        out_specs=pl.BlockSpec((slots, wide), lambda i: (0, 0)),
        compiler_params=pltpu.CompilerParams(vmem_limit_bytes=48 * 2**20),
    )(arrived, arrived, arrived, weight, refs, refs, refs)


def pick_kernel(slot_ref, table_ref, lists_ref, out_ref, rows_ref):
    count, entries = lists_ref.shape
    wide = table_ref.shape[1]

    @pl.loop(0, count)
    def _(i):
        rows_ref[pl.ds(i, 1), :] = table_ref[pl.ds(slot_ref[i], 1), :]

    lists = lists_ref[...]
    place = lists % entries
    value = jnp.zeros((count, entries), jnp.float32)
    for b in range(wide // entries):
        here = jnp.take_along_axis(rows_ref[:, b * entries : (b + 1) * entries], place, axis=1)
        value = jnp.where(lists // entries == b, here, value)
    out_ref[...] = value - jnp.mean(value, axis=1, keepdims=True)


def pick(slot, table, lists):
    vmem = pl.BlockSpec(memory_space=pltpu.VMEM)
    return pl.pallas_call(
        pick_kernel,
        out_shape=jax.ShapeDtypeStruct(lists.shape, jnp.float32),
        in_specs=[pl.BlockSpec(memory_space=pltpu.SMEM), vmem, vmem],
        out_specs=vmem,
        scratch_shapes=[pltpu.VMEM((lists.shape[0], table.shape[1]), jnp.float32)],
    )(slot, table, lists)


def per_device_routed(images, ctf, shifts, home, neighbours, references, noise_weight):
    groups = lax.axis_size("grp")
    owners = lax.axis_size("orient")
    local, _, pixels = images.shape
    slots = max(2, 2 * local // owners)
    core = lax.axis_index("orient") % 2
    target = home[:, :, 0]
    earlier = jnp.arange(local)[None, :] < jnp.arange(local)[:, None]
    rank = jnp.sum(((target[:, :, None] == target[:, None, :]) & earlier[None]).astype(jnp.int32), axis=2)
    marks = (target * 2 + core) * slots + rank
    lane = jnp.arange(128, dtype=jnp.int32)
    marks = jnp.where(
        (lane // local == core)[None, :], jnp.tile(marks, (1, 128 // local)), -1
    )
    marks = jnp.pad(marks, ((0, -groups % 8), (0, 0)), constant_values=-1)
    payload = shift(images, ctf, shifts)
    arrived, flat = route(marks, payload, references[0], groups, owners // 2, 2 * slots)
    table = score(arrived, noise_weight, flat, 1024)
    returned = lax.all_to_all(
        table.reshape(groups * owners, slots, -1), ("grp", "orient"), split_axis=0, concat_axis=0, tiled=True
    )
    slot = (jnp.arange(groups, dtype=jnp.int32)[:, None] * owners + target) * slots + rank
    entries = neighbours.shape[2]
    return pick(
        slot.T.reshape(-1),
        returned.reshape(groups * owners * slots, -1),
        neighbours.reshape(local * groups, entries),
    ).reshape(neighbours.shape)


def per_device(images, ctf, shifts, home, neighbours, references, noise_weight):
    owners = lax.axis_size("orient")
    local = images.shape[0]
    slots = max(2, 2 * local // owners)
    parts = images.shape[2] // 512
    long = parts >= (owners // 2 - 1) * CHUNKS and images.shape[2] % 2048 == 0
    routed = long and owners % 2 == 0 and slots % 8 == 0 and local % 16 == 0 and 128 % (2 * local) == 0
    form = per_device_routed if routed else per_device_plain
    return form(images, ctf, shifts, home, neighbours, references, noise_weight)


def solution(mesh):
    in_specs = (
        P(("grp", "orient"), None, None),
        P(("grp", "orient"), None),
        P(("grp", "orient"), None),
        P(None, ("grp", "orient"), None),
        P(("grp", "orient"), None, None),
        P("grp", "orient", None, None),
        P("grp", None),
    )
    out_specs = P(("grp", "orient"), None, None)
    return jax.shard_map(
        per_device, mesh=mesh, in_specs=in_specs, out_specs=out_specs, check_vma=False
    )
```
